32 devices in a mesh: tok: 8 (over z, x), head: 4 (over y, core).
Axes of the slice: x: 2, y: 2, z: 4, core: 2. Of those that a mesh axis runs over, the one named last changes fastest.
Arguments:
- head_inputs: bfloat16 [4096, 2048], P('tok', 'head'), may hold values from -6 to 6
- state_keys: bfloat16 [4096, 128], P('tok'), may hold values from -2 to 2
- state_queries: bfloat16 [4096, 128], P('tok'), may hold values from -2 to 2
- log_decay: float32 [4096, 32], P('tok', 'head'), may hold values from -1.6 to 0, as said below
- level_weight: float32 [4096, 32, 18], P('tok', 'head'), may hold values from 0.2 to 2
- skip_scale: float32 [32], P('head'), may hold values from 0.5 to 2
- gate_input: bfloat16 [4096, 2048], P('tok', 'head'), may hold values from -500 to 500
- norm_gain: float32 [2048], P('head'), may hold values from 0.5 to 1.5
Outputs:
- mixer_out: bfloat16 [4096, 2048], P('tok', 'head')
The draws below stay inside these ranges and needn't reach their ends.
Inputs may be any that keep to these rules, and one draw needn't show every extreme that they name: `log_decay`: every entry is negative.
All inputs are finite; a program needn't handle non-finite values.
Results may differ from the reference program's by a relative error of at most 0.0038.
Values sent between devices are 32-bit elements; how exact they have to be, the bound alone decides.
A program may use at most 64 MiB of HBM per device.

```python
import math
import jax
import jax.numpy as jnp
import numpy as np
from jax import lax

HEAD_TOTAL = 32
HEAD_DIM = 64
STATE_DIM = 128
TOK_DEV = 512
LEVELS = 18
TOKEN_TOTAL = 4096


def draw_log_decay(key, part):
    sequence_flows = jax.random.split(key, 7)
    slow_share = 0.5
    slow_heads = jax.random.uniform(sequence_flows[0], (HEAD_TOTAL,), jnp.float32) < slow_share
    fast_rate = jnp.exp(jax.random.uniform(sequence_flows[1], (HEAD_TOTAL,), jnp.float32, math.log(1.0 / 110.0), math.log(1.0 / 100.0)))
    slow_rate = jnp.exp(jax.random.uniform(sequence_flows[2], (HEAD_TOTAL,), jnp.float32, math.log(0.1), 0.0)) * math.log(10.0) / (8.0 * TOKEN_TOTAL)
    rate = jnp.where(slow_heads, slow_rate, fast_rate)
    roughness = jax.random.uniform(sequence_flows[3], (TOKEN_TOTAL, HEAD_TOTAL), jnp.float32, 0.5, 1.5)
    block_factor = jax.random.uniform(sequence_flows[4], (TOKEN_TOTAL // TOK_DEV, HEAD_TOTAL), jnp.float32, 1.0, 1.2)
    block_factor = jnp.repeat(block_factor, TOK_DEV, axis=0)
    baseline_level = -rate[None, :] * roughness * block_factor
    spike_location = jax.random.randint(sequence_flows[5], (2,), 0, TOKEN_TOTAL)
    spike_value = jnp.log(jax.random.uniform(sequence_flows[6], (2, HEAD_TOTAL), jnp.float32, 0.5, 0.8))
    spike_flagged = (jnp.arange(TOKEN_TOTAL, dtype=jnp.int32)[:, None] == spike_location[None, :]).astype(jnp.float32)
    return (baseline_level + jnp.dot(spike_flagged, spike_value)).astype(jnp.float32)


def draw_gate_input(key, part):
    sequence_flows = jax.random.split(key, 3)
    columns = HEAD_TOTAL * HEAD_DIM
    column_scale = jnp.exp(math.log(3.0) * jnp.arange(columns, dtype=jnp.float32) / columns + jax.random.uniform(sequence_flows[0], (columns,), jnp.float32, 0.0, math.log(10.0)))
    row_scale = jnp.exp(jax.random.uniform(sequence_flows[1], (TOKEN_TOTAL, 1), jnp.float32, 0.0, math.log(4.0)))
    base_draw = jnp.clip(jax.random.normal(sequence_flows[2], (TOKEN_TOTAL, columns), jnp.float32), -4.0, 4.0)
    return (base_draw * row_scale * column_scale[None, :]).astype(jnp.bfloat16)


def steps_of(stream_key, extent, cuts, low, largest):
    gain, own = 1.0, jax.random.fold_in(stream_key, 6)
    for position, blocks in cuts:
        steps = jnp.exp(jax.random.uniform(jax.random.fold_in(own, position), (blocks,), jnp.float32, low / len(cuts), largest / len(cuts)))
        gain = gain * jnp.repeat(steps, extent[position] // blocks).reshape([-1 if axis == position else 1 for axis in range(len(extent))])
    return gain


def scatter_about(key, extent, deviation, most, cuts=(), kind=jnp.bfloat16):
    values = jax.random.normal(key, extent, jnp.float32) * deviation
    if len(cuts) > 0:
        values = steps_of(key, extent, cuts, -0.22, 0.18) * values
    return jnp.clip(values, min=-most, max=most).astype(kind)


def setup_inputs(seed: int = 0) -> dict:
    key_of = jax.random.split(jax.random.key(seed), 9)
    head_inputs = scatter_about(key_of[0], (TOKEN_TOTAL, HEAD_TOTAL * HEAD_DIM), 1.0, 6.0, ((0, 8), (1, 4)))
    state_keys = scatter_about(key_of[1], (TOKEN_TOTAL, STATE_DIM), 0.3, 2.0, ((0, 8),))
    state_queries = scatter_about(key_of[2], (TOKEN_TOTAL, STATE_DIM), 0.3, 2.0, ((0, 8),))
    log_decay = draw_log_decay(jax.random.fold_in(key_of[8], 71), 0)
    level_weight = jnp.clip(jnp.exp(math.log(2.0) - 2.3025851 * jax.random.uniform(key_of[4], (TOKEN_TOTAL, HEAD_TOTAL, LEVELS), jnp.float32) ** steps_of(key_of[4], (TOKEN_TOTAL, HEAD_TOTAL, LEVELS), ((0, 8), (1, 4)), -0.2, 0.2)), 0.2, 2.0)
    skip_scale = jnp.clip(0.5 + 1.5 * jax.random.uniform(key_of[5], (HEAD_TOTAL,), jnp.float32) ** steps_of(key_of[5], (HEAD_TOTAL,), ((0, 4),), -0.2, 0.2), 0.5, 2.0)
    gate_input = draw_gate_input(jax.random.fold_in(key_of[8], 71), 0)
    norm_gain = jnp.clip(0.5 + 1.0 * jax.random.uniform(key_of[7], (HEAD_TOTAL * HEAD_DIM,), jnp.float32) ** steps_of(key_of[7], (HEAD_TOTAL * HEAD_DIM,), ((0, 4),), -0.2, 0.2), 0.5, 1.5)
    return dict(head_inputs=head_inputs, state_keys=state_keys, state_queries=state_queries, log_decay=log_decay, level_weight=level_weight, skip_scale=skip_scale, gate_input=gate_input, norm_gain=norm_gain)


def block_levels(first_row, row_count, col_count, local_bits):
    query_pos = first_row + jnp.arange(row_count, dtype=jnp.int32)
    key_pos = jnp.arange(col_count, dtype=jnp.int32)
    crossing = jnp.bitwise_xor(query_pos[:, None], key_pos[None, :])
    level_map = jnp.zeros((row_count, col_count), jnp.int32)
    for shift_bit in range(local_bits):
        level_map = level_map + (crossing >= 1 << shift_bit).astype(jnp.int32)
    return (level_map, key_pos[None, :] <= query_pos[:, None])

def local_mix(queries, key_rows, values, decays, scales, local_bits):
    block_len = queries.shape[0]
    row_block = min(512, block_len)
    pieces_out = []
    for first_row in range(0, block_len, row_block):
        last_row = first_row + row_block
        scores = jnp.dot(queries[first_row:last_row], key_rows[:last_row].T, preferred_element_type=jnp.float32)
        level_map, causal = block_levels(first_row, row_block, last_row, local_bits)

        def one_head(inputs):
            decay_row, scale_row, value_row = inputs
            spread = jnp.where(causal, decay_row[first_row:last_row, None] - decay_row[None, :last_row], -jnp.inf)
            chosen = jnp.zeros((row_block, last_row), jnp.float32)
            for level_index in range(local_bits + 1):
                chosen = chosen + jnp.where(level_map == level_index, scale_row[first_row:last_row, level_index:level_index + 1], 0.0)
            weighted = (scores * jnp.exp(spread) * chosen).astype(jnp.bfloat16)
            return jnp.dot(weighted, value_row[:last_row], preferred_element_type=jnp.float32)
        pieces_out.append(lax.map(one_head, (decays, scales, values)))
    return jnp.concatenate(pieces_out, axis=1)

def make_state(key_rows, values, decays):
    scaled = (key_rows.astype(jnp.float32)[None] * jnp.exp(decays[:, -1:] - decays)[:, :, None]).astype(jnp.bfloat16)
    return jnp.einsum('htn,htp->hnp', scaled.astype(jnp.float32), values.astype(jnp.float32), precision=lax.Precision.HIGHEST)

def far_mix(queries, decays, scales, crossed, first_level):
    query_wide = queries.astype(jnp.float32)
    tree_bits = crossed.shape[1]

    def one_head(inputs):
        decay_row, scale_row, state_row = inputs
        stacked = state_row.transpose(1, 0, 2).reshape(state_row.shape[1], -1)
        readout = jnp.dot(query_wide, stacked, precision=lax.Precision.HIGHEST).reshape(query_wide.shape[0], tree_bits, -1)
        level_scale = scale_row[:, first_level:first_level + tree_bits]
        return jnp.exp(decay_row)[:, None] * lax.optimization_barrier(jnp.sum(level_scale[:, :, None] * readout, axis=1))
    return lax.map(one_head, (decays, scales, crossed))

def head_mix(queries, key_rows, values, decays, scales, crossed, gates, skip_scale, local_bits):
    nearby = local_mix(queries, key_rows, values, decays, scales, local_bits)
    distant = far_mix(queries, decays, scales, crossed, local_bits + 1)
    mixed_out = nearby + distant + skip_scale[:, None, None] * values.astype(jnp.float32)
    head_count, block_len, head_size = mixed_out.shape
    mixed_out = mixed_out.transpose(1, 0, 2).reshape(block_len, head_count * head_size)
    return mixed_out * jax.nn.silu(gates.astype(jnp.float32))

def reference(head_inputs, state_keys, state_queries, log_decay, level_weight, skip_scale, gate_input, norm_gain):
    block_count = TOKEN_TOTAL // TOK_DEV
    local_bits = TOK_DEV.bit_length() - 1
    tree_bits = block_count.bit_length() - 1
    head_values = head_inputs.reshape(block_count, TOK_DEV, HEAD_TOTAL, HEAD_DIM).transpose(0, 2, 1, 3)
    decay_sum = jnp.cumsum(log_decay.reshape(block_count, TOK_DEV, HEAD_TOTAL), axis=1).transpose(0, 2, 1)
    weights = level_weight.reshape(block_count, TOK_DEV, HEAD_TOTAL, LEVELS).transpose(0, 2, 1, 3)
    key_blocks = state_keys.reshape(block_count, TOK_DEV, STATE_DIM)
    query_blocks = state_queries.reshape(block_count, TOK_DEV, STATE_DIM)
    gate_blocks = gate_input.reshape(block_count, TOK_DEV, HEAD_TOTAL * HEAD_DIM)

    def state_block(inputs):
        return make_state(inputs[0], inputs[1], inputs[2])
    states = lax.map(state_block, (key_blocks, head_values, decay_sum))
    totals = decay_sum[:, :, -1]
    collected = []
    for level_bit in range(tree_bits):
        group_size = 1 << level_bit
        group_totals = totals.reshape(block_count // group_size, group_size, HEAD_TOTAL)
        after_sum = jnp.cumsum(group_totals[:, ::-1], axis=1)[:, ::-1] - group_totals
        before_sum = jnp.cumsum(group_totals, axis=1) - group_totals
        group_states = states.reshape(block_count // group_size, group_size, HEAD_TOTAL, STATE_DIM, HEAD_DIM)
        merged = lax.optimization_barrier(jnp.sum(group_states * jnp.exp(after_sum)[:, :, :, None, None], axis=1))
        group_index = np.arange(block_count) // group_size
        upper_half = group_index % 2 == 1
        sibling = np.maximum(group_index - 1, 0)
        picked = merged[sibling] * jnp.exp(before_sum.reshape(block_count, HEAD_TOTAL))[:, :, None, None]
        collected.append(jnp.where(jnp.asarray(upper_half)[:, None, None, None], picked, 0.0))
    crossed = jnp.stack(collected, axis=2)

    def one_block(inputs):
        queries, key_rows, values, decays, scales, states_here, gates = inputs
        gated_out = head_mix(queries, key_rows, values, decays, scales, states_here, gates, skip_scale, local_bits)
        squares = lax.optimization_barrier(jnp.mean(gated_out * gated_out, axis=1, keepdims=True))
        return (gated_out * lax.rsqrt(squares + 1e-05) * norm_gain).astype(jnp.bfloat16)
    result = lax.map(one_block, (query_blocks, key_blocks, head_values, decay_sum, weights, crossed, gate_blocks))
    return result.reshape(TOKEN_TOTAL, HEAD_TOTAL * HEAD_DIM)
```

```python
import functools

import jax
import jax.numpy as jnp
from jax import lax
from jax.experimental import pallas as pl
from jax.experimental.pallas import tpu as pltpu
from jax.sharding import PartitionSpec as P

epsilon = 1e-05
F32, BF16 = jnp.float32, jnp.bfloat16
MESH = pl.DeviceIdType.MESH


def dot(a, b):
    return jnp.dot(a, b, preferred_element_type=F32)


def dot_t(a, b):
    return lax.dot_general(a, b, (((1,), (1,)), ((), ())), preferred_element_type=F32)


def bit_of(value, b):
    return lax.rem(lax.div(value, 1 << b), 2) == 1


def column(row, size):
    return jnp.broadcast_to(row, (size, size)).T


def level_of(crossing, bits):
    level = jnp.zeros(crossing.shape, jnp.int32)
    for b in range(bits):
        level = level + (crossing >= 1 << b).astype(jnp.int32)
    return level


def kernel(
    sizes,
    x_ref, k_ref, q_ref, ld_ref, w_ref, skip_ref, gate_ref, gain_ref,
    out_ref,
    d_ref, tot, fac_lead, fac_all, state, agg, got, base, sg, vt, gt, kt, qq, score, turned, ssq,
    tot_send, tot_recv, st_send, st_recv, sq_send, sq_recv,
):
    toks, heads_ax, tile, chunks = sizes
    block, width = x_ref.shape
    heads = ld_ref.shape[0]
    size = width // heads
    local_bits = block.bit_length() - 1
    tree = toks.bit_length() - 1
    tiles = block // tile
    tile_bits = tile.bit_length() - 1
    per = heads // chunks
    rows = per * size
    me = lax.axis_index("tok")
    my_head = lax.axis_index("head")
    odd = lax.rem(me, 2) == 1
    partner = me + 1 - 2 * lax.rem(me, 2)

    barrier = pltpu.get_barrier_semaphore()
    for i in range(1, toks):
        pl.semaphore_signal(barrier, inc=1, device_id={"tok": lax.rem(me + i, toks)}, device_id_type=MESH)
    for i in range(1, heads_ax):
        pl.semaphore_signal(barrier, inc=1, device_id={"head": lax.rem(my_head + i, heads_ax)}, device_id_type=MESH)

    ones = (
        lax.broadcasted_iota(jnp.int32, (tile, tile), 0) <= lax.broadcasted_iota(jnp.int32, (tile, tile), 1)
    ).astype(F32)
    inside = jnp.dot(
        jnp.concatenate([ld_ref[:, i * tile : (i + 1) * tile] for i in range(tiles)], axis=0),
        ones, precision=lax.Precision.HIGHEST, preferred_element_type=F32,
    )
    run = jnp.zeros((heads, 1), F32)
    for i in range(tiles):
        part = inside[i * heads : (i + 1) * heads] + run
        d_ref[:, i * tile : (i + 1) * tile] = part
        run = part[:, tile - 1 :]
    tot[me] = jnp.broadcast_to(run, tot.shape[1:])
    pl.semaphore_wait(barrier, toks - 1 + heads_ax - 1)

    def tot_copy(peer, slot):
        return pltpu.make_async_remote_copy(
            src_ref=tot.at[slot], dst_ref=tot.at[slot], send_sem=tot_send.at[peer], recv_sem=tot_recv.at[slot],
            device_id={"tok": peer}, device_id_type=MESH,
        )

    for i in range(1, toks):
        tot_copy(lax.rem(me + i, toks), me).start()

    def state_copy(src, b, c, peer):
        part = pl.ds(c * rows, rows)
        return pltpu.make_async_remote_copy(
            src_ref=src.at[part], dst_ref=got.at[b, part], send_sem=st_send.at[b, c], recv_sem=st_recv.at[b, c],
            device_id={"tok": peer}, device_id_type=MESH,
        )

    vt[...] = x_ref[...].T
    kt[...] = k_ref[...].T.astype(F32)
    to_end = jnp.exp(run - d_ref[...])
    for c in range(chunks):
        for h in range(c * per, (c + 1) * per):
            scaled = (kt[...] * to_end[h : h + 1]).astype(BF16)
            state[h * size : (h + 1) * size] = dot_t(vt[h * size : (h + 1) * size], scaled)
        state_copy(state, 0, c, partner).start()

    gt[...] = gate_ref[...].T
    qt = q_ref[...].T
    depth = qt.shape[0]
    qq[:depth] = qt
    qq[depth:] = qt
    score[...] = dot_t(k_ref[...], q_ref[...])

    groups = tile // 8
    t_at = lax.broadcasted_iota(jnp.int32, (groups, tile), 1)
    g_at = lax.broadcasted_iota(jnp.int32, (groups, tile), 0)
    coarse = jnp.where(t_at // 8 > g_at, level_of((t_at // 8) ^ g_at, tile_bits - 3) + 3, -1)
    same = (t_at // 8 == g_at).astype(F32).reshape(groups, 1, tile) > 0.5
    r_at = lax.broadcasted_iota(jnp.int32, (8, tile), 0)
    u_at = lax.broadcasted_iota(jnp.int32, (8, tile), 1) % 8
    fine = jnp.where(u_at >= r_at, level_of(u_at ^ r_at, 3), -1)

    def near(h, _):
        lines = pl.ds(pl.multiple_of(h * size, size), size)
        decay = d_ref[pl.ds(h, 1), :]
        weight = [w_ref[l, pl.ds(h, 1), :] for l in range(local_bits + 1)]
        cut = [slice(i * tile, (i + 1) * tile) for i in range(tiles)]
        made = {}
        for j in range(tiles):
            at_s = column(decay[:, cut[j]], tile)
            rough = jnp.zeros((groups, tile), F32)
            for l in range(4, tile_bits + 1):
                rough = jnp.where(coarse == l, weight[l][:, cut[j]], rough)
            exact = jnp.zeros((8, tile), F32)
            for l in range(4):
                exact = jnp.where(fine == l, weight[l][:, cut[j]], exact)
            chosen = jnp.where(
                jnp.broadcast_to(same, (groups, 8, tile)),
                jnp.broadcast_to(exact[None], (groups, 8, tile)),
                jnp.broadcast_to(rough[:, None, :], (groups, 8, tile)),
            ).reshape(tile, tile)
            spread = jnp.exp(jnp.minimum(decay[:, cut[j]] - at_s, 0.0))
            made[j, j] = (score[cut[j], cut[j]] * spread * chosen).astype(BF16)
            if j + 1 < tiles:
                last = decay[:, (j + 1) * tile - 1 : (j + 1) * tile]
                fall = jnp.exp(last - at_s)
                for i in range(j + 1, tiles):
                    by = weight[(i ^ j).bit_length() + tile_bits][:, cut[i]] * jnp.exp(decay[:, cut[i]] - last)
                    made[j, i] = (score[cut[j], cut[i]] * fall * by).astype(BF16)
        v = vt[lines, :]
        parts = []
        empty = jnp.zeros((tile, tile), BF16)
        pair = min(2, tiles)
        for i in range(0, tiles, pair):
            cols = [
                jnp.concatenate([made.get((j, ii), empty) for j in range(i + pair)], axis=0)
                for ii in range(i, i + pair)
            ]
            parts.append(dot(v[:, : (i + pair) * tile], jnp.concatenate(cols, axis=1)))
        g = gt[lines, :].astype(F32)
        g = g / (1.0 + jnp.exp(-g))
        sg[lines, :] = g
        base[lines, :] = (jnp.concatenate(parts, axis=1) + skip_ref[h] * v.astype(F32)) * g
        return 0

    def receives(b):
        return bit_of(me, b)

    def sends(b):
        return jnp.logical_and(me + 2 < toks, bit_of(me + 2, b))

    def all_ones(first, last):
        value = me >= 0
        for b in range(first, last):
            value = jnp.logical_and(value, bit_of(me, b))
        return value

    def send_own(b, c):
        if b < tree:

            @pl.when(jnp.logical_and(jnp.logical_not(bit_of(me, b)), jnp.logical_and(sends(b), all_ones(1, b))))
            def _():
                state_copy(agg, b, c, lax.rem(me + 2, toks)).start()

    def comm(b, c):
        def each(fn):
            for h in range(c * per, (c + 1) * per):
                fn(h, slice(h * size, (h + 1) * size))

        if b == 0:
            state_copy(state, 0, c, partner).wait_recv()

            def join(h, s):
                mine, other = state[s], got[0, s]
                agg[s] = jnp.where(odd, other, mine) * fac_all[0, h : h + 1, :] + jnp.where(odd, mine, other)

            if tree > 1:
                each(join)
            send_own(1, c)
        else:

            @pl.when(receives(b))
            def _():
                state_copy(agg, b, c, lax.rem(me + 2, toks)).wait_recv()

                @pl.when(sends(b))
                def _():
                    state_copy(got.at[b], b, c, lax.rem(me + 2, toks)).start()

                if b + 1 < tree:

                    @pl.when(all_ones(1, b + 1))
                    def _():
                        def join(h, s):
                            agg[s] = got[b, s] * fac_all[b, h : h + 1, :] + agg[s]

                        each(join)
                        send_own(b + 1, c)

    def distant(b, c):
        @pl.when(receives(b))
        def _():
            s = slice(c * rows, (c + 1) * rows)
            lead = jnp.concatenate(
                [jnp.broadcast_to(fac_lead[b, h : h + 1, :], (size, depth)) for h in range(c * per, (c + 1) * per)], 0
            )
            x = got[b, s] * lead
            high = x.astype(BF16)
            low = (x - high.astype(F32)).astype(BF16)
            read = dot(jnp.concatenate([high, low], axis=1), qq[...])
            for h in range(per):
                hh = c * per + h
                by = w_ref[local_bits + 1 + b, hh : hh + 1, :] * jnp.exp(d_ref[hh : hh + 1, :])
                o = slice(hh * size, (hh + 1) * size)
                base[o] += read[h * size : (h + 1) * size] * by * sg[o]

    for k in range(chunks + tree - 1):
        if k < chunks:
            lax.fori_loop(k * per, (k + 1) * per, near, 0)
        if k == 0:
            for i in range(1, toks):
                tot_copy(me, lax.rem(me + i, toks)).wait_recv()
            for b in range(tree):
                start = lax.div(me, 1 << b) * (1 << b)
                lead = jnp.zeros(tot.shape[1:], F32)
                full = lead
                low = start if b else me + 1 - lax.rem(me, 2)
                for m in range(toks):
                    one = tot[m]
                    lead = lead + jnp.where(jnp.logical_and(m >= start, m < me), one, 0.0)
                    full = full + jnp.where(jnp.logical_and(m >= low, m < low + (1 << b)), one, 0.0)
                fac_lead[b] = jnp.exp(lead)
                fac_all[b] = jnp.exp(full)
        for b in range(tree):
            if 0 <= k - b < chunks:
                comm(b, k - b)
        for b in range(tree):
            if 0 <= k - b < chunks:
                distant(b, k - b)

    total = jnp.zeros((1, block), F32)
    for h in range(heads):
        g = base[h * size : (h + 1) * size]
        total = total + jnp.sum(g * g, axis=0, keepdims=True)
    ssq[my_head] = total

    def sq_copy(peer, slot):
        return pltpu.make_async_remote_copy(
            src_ref=ssq.at[slot], dst_ref=ssq.at[slot], send_sem=sq_send.at[peer], recv_sem=sq_recv.at[slot],
            device_id={"head": peer}, device_id_type=MESH,
        )

    for i in range(1, heads_ax):
        sq_copy(lax.rem(my_head + i, heads_ax), my_head).start()
    turned[...] = base[...].T * gain_ref[...]
    for i in range(1, heads_ax):
        sq_copy(my_head, lax.rem(my_head + i, heads_ax)).wait_recv()
    squares = ssq[0]
    for m in range(1, heads_ax):
        squares = squares + ssq[m]
    scaling = lax.rsqrt(squares / (width * heads_ax) + epsilon)
    for i in range(tiles):
        s = slice(i * tile, (i + 1) * tile)
        by = column(scaling[:, s], tile)
        for j in range(width // tile):
            c = slice(j * tile, (j + 1) * tile)
            out_ref[s, c] = (turned[s, c] * by).astype(BF16)

    for i in range(1, toks):
        tot_copy(lax.rem(me + i, toks), me).wait_send()
    for i in range(1, heads_ax):
        sq_copy(lax.rem(my_head + i, heads_ax), my_head).wait_send()
    for c in range(chunks):
        state_copy(state, 0, c, partner).wait_send()
    for b in range(1, tree):

        @pl.when(jnp.logical_and(sends(b), jnp.logical_or(bit_of(me, b), all_ones(1, b))))
        def _():
            for c in range(chunks):
                state_copy(agg, b, c, lax.rem(me + 2, toks)).wait_send()


def shards(toks, heads_ax, x, k, q, ld, w, skip, gate, gain):
    block, width = x.shape
    heads = ld.shape[1]
    depth = k.shape[1]
    tree = toks.bit_length() - 1
    tile = 128
    chunks = min(4, heads)
    vmem = pl.BlockSpec(memory_space=pltpu.VMEM)
    return pl.pallas_call(
        functools.partial(kernel, (toks, heads_ax, tile, chunks)),
        out_shape=jax.ShapeDtypeStruct((block, width), BF16),
        in_specs=[vmem] * 5 + [pl.BlockSpec(memory_space=pltpu.SMEM)] + [vmem] * 2,
        out_specs=vmem,
        scratch_shapes=[
            pltpu.VMEM((heads, block), F32),
            pltpu.VMEM((toks, heads, depth), F32),
            pltpu.VMEM((tree, heads, depth), F32),
            pltpu.VMEM((tree, heads, depth), F32),
            pltpu.VMEM((width, depth), F32),
            pltpu.VMEM((width, depth), F32),
            pltpu.VMEM((tree, width, depth), F32),
            pltpu.VMEM((width, block), F32),
            pltpu.VMEM((width, block), F32),
            pltpu.VMEM((width, block), BF16),
            pltpu.VMEM((width, block), BF16),
            pltpu.VMEM((depth, block), F32),
            pltpu.VMEM((2 * depth, block), BF16),
            pltpu.VMEM((block, block), F32),
            pltpu.VMEM((block, width), F32),
            pltpu.VMEM((heads_ax, 1, block), F32),
            pltpu.SemaphoreType.DMA((toks,)),
            pltpu.SemaphoreType.DMA((toks,)),
            pltpu.SemaphoreType.DMA((tree, chunks)),
            pltpu.SemaphoreType.DMA((tree, chunks)),
            pltpu.SemaphoreType.DMA((heads_ax,)),
            pltpu.SemaphoreType.DMA((heads_ax,)),
        ],
        compiler_params=pltpu.CompilerParams(
            collective_id=0, has_side_effects=True, vmem_limit_bytes=40 * 2**20
        ),
    )(x, k, q, ld.T, w.transpose(2, 1, 0), skip, gate, gain[None, :])


def solution(mesh):
    return jax.shard_map(
        functools.partial(shards, mesh.shape["tok"], mesh.shape["head"]),
        mesh=mesh,
        in_specs=(
            P("tok", "head"),
            P("tok", None),
            P("tok", None),
            P("tok", "head"),
            P("tok", "head", None),
            P("head"),
            P("tok", "head"),
            P("head"),
        ),
        out_specs=P("tok", "head"),
        check_vma=False,
    )
```

```python
import functools

import jax
import jax.numpy as jnp
from jax import lax
from jax.experimental import pallas as pl
from jax.experimental.pallas import tpu as pltpu
from jax.sharding import PartitionSpec as P

epsilon = 1e-05
F32, BF16 = jnp.float32, jnp.bfloat16
MESH = pl.DeviceIdType.MESH


def dot(a, b):
    return jnp.dot(a, b, preferred_element_type=F32)


def dot_t(a, b):
    return lax.dot_general(a, b, (((1,), (1,)), ((), ())), preferred_element_type=F32)


def bit_of(value, b):
    return lax.rem(lax.div(value, 1 << b), 2) == 1


def column(row, size):
    return jnp.broadcast_to(row, (size, size)).T


def level_of(crossing, bits):
    level = jnp.zeros(crossing.shape, jnp.int32)
    for b in range(bits):
        level = level + (crossing >= 1 << b).astype(jnp.int32)
    return level


def kernel(
    sizes,
    x_in, k_in, q_in, ld_in, w_in, skip_ref, gate_in, gain_ref,
    out_ref,
    x_ref, k_ref, q_ref, ld_ref, w_ref, gate_ref, load_sem,
    d_ref, tot, fac_lead, fac_all, state, agg, got, base, sg, vt, gt, kt, qq, score, turned, ssq,
    tot_send, tot_recv, st_send, st_recv, sq_send, sq_recv,
):
    toks, heads_ax, tile, chunks = sizes
    loads = {
        name: pltpu.make_async_copy(src, dst, load_sem.at[i])
        for i, (name, src, dst) in enumerate(
            (
                ("ld", ld_in, ld_ref), ("k", k_in, k_ref), ("x", x_in, x_ref),
                ("q", q_in, q_ref), ("gate", gate_in, gate_ref), ("w", w_in, w_ref),
            )
        )
    }
    for load in loads.values():
        load.start()
    block, width = x_ref.shape
    heads = ld_ref.shape[0]
    size = width // heads
    local_bits = block.bit_length() - 1
    tree = toks.bit_length() - 1
    tiles = block // tile
    tile_bits = tile.bit_length() - 1
    per = heads // chunks
    rows = per * size
    me = lax.axis_index("tok")
    my_head = lax.axis_index("head")
    odd = lax.rem(me, 2) == 1
    partner = me + 1 - 2 * lax.rem(me, 2)

    barrier = pltpu.get_barrier_semaphore()
    for i in range(1, toks):
        pl.semaphore_signal(barrier, inc=1, device_id={"tok": lax.rem(me + i, toks)}, device_id_type=MESH)
    for i in range(1, heads_ax):
        pl.semaphore_signal(barrier, inc=1, device_id={"head": lax.rem(my_head + i, heads_ax)}, device_id_type=MESH)

    with jax.named_scope("running_sum"):
        loads["ld"].wait()
        ones = (
            lax.broadcasted_iota(jnp.int32, (tile, tile), 0) <= lax.broadcasted_iota(jnp.int32, (tile, tile), 1)
        ).astype(F32)
        inside = jnp.dot(
            jnp.concatenate([ld_ref[:, i * tile : (i + 1) * tile] for i in range(tiles)], axis=0),
            ones, precision=lax.Precision.HIGHEST, preferred_element_type=F32,
        )
        run = jnp.zeros((heads, 1), F32)
        for i in range(tiles):
            part = inside[i * heads : (i + 1) * heads] + run
            d_ref[:, i * tile : (i + 1) * tile] = part
            run = part[:, tile - 1 :]

    tot[me] = jnp.broadcast_to(run, tot.shape[1:])
    with jax.named_scope("barrier"):
        pl.semaphore_wait(barrier, toks - 1 + heads_ax - 1)

    def tot_copy(peer, slot):
        return pltpu.make_async_remote_copy(
            src_ref=tot.at[slot], dst_ref=tot.at[slot], send_sem=tot_send.at[peer], recv_sem=tot_recv.at[slot],
            device_id={"tok": peer}, device_id_type=MESH,
        )

    for i in range(1, toks):
        tot_copy(lax.rem(me + i, toks), me).start()

    def state_copy(src, b, c, peer):
        part = pl.ds(c * rows, rows)
        return pltpu.make_async_remote_copy(
            src_ref=src.at[part], dst_ref=got.at[b, part], send_sem=st_send.at[b, c], recv_sem=st_recv.at[b, c],
            device_id={"tok": peer}, device_id_type=MESH,
        )

    with jax.named_scope("states"):
        loads["k"].wait()
        loads["x"].wait()
        vt[...] = x_ref[...].T
        kt[...] = k_ref[...].T.astype(F32)
        to_end = jnp.exp(run - d_ref[...])
        for c in range(chunks):
            for h in range(c * per, (c + 1) * per):
                scaled = (kt[...] * to_end[h : h + 1]).astype(BF16)
                state[h * size : (h + 1) * size] = dot_t(vt[h * size : (h + 1) * size], scaled)
            state_copy(state, 0, c, partner).start()

    with jax.named_scope("scores"):
        loads["gate"].wait()
        gt[...] = gate_ref[...].T
        loads["q"].wait()
        loads["w"].wait()
        qt = q_ref[...].T
        depth = qt.shape[0]
        qq[:depth] = qt
        qq[depth:] = qt
        score[...] = dot_t(k_ref[...], q_ref[...])

    groups = tile // 8
    t_at = lax.broadcasted_iota(jnp.int32, (groups, tile), 1)
    g_at = lax.broadcasted_iota(jnp.int32, (groups, tile), 0)
    coarse = jnp.where(t_at // 8 > g_at, level_of((t_at // 8) ^ g_at, tile_bits - 3) + 3, -1)
    same = (t_at // 8 == g_at).astype(F32).reshape(groups, 1, tile) > 0.5
    r_at = lax.broadcasted_iota(jnp.int32, (8, tile), 0)
    u_at = lax.broadcasted_iota(jnp.int32, (8, tile), 1) % 8
    fine = jnp.where(u_at >= r_at, level_of(u_at ^ r_at, 3), -1)

    def near(h, _):
        lines = pl.ds(pl.multiple_of(h * size, size), size)
        decay = d_ref[pl.ds(h, 1), :]
        weight = [w_ref[l, pl.ds(h, 1), :] for l in range(local_bits + 1)]
        cut = [slice(i * tile, (i + 1) * tile) for i in range(tiles)]
        made = {}
        for j in range(tiles):
            at_s = column(decay[:, cut[j]], tile)
            rough = jnp.zeros((groups, tile), F32)
            for l in range(4, tile_bits + 1):
                rough = jnp.where(coarse == l, weight[l][:, cut[j]], rough)
            exact = jnp.zeros((8, tile), F32)
            for l in range(4):
                exact = jnp.where(fine == l, weight[l][:, cut[j]], exact)
            chosen = jnp.where(
                jnp.broadcast_to(same, (groups, 8, tile)),
                jnp.broadcast_to(exact[None], (groups, 8, tile)),
                jnp.broadcast_to(rough[:, None, :], (groups, 8, tile)),
            ).reshape(tile, tile)
            spread = jnp.exp(jnp.minimum(decay[:, cut[j]] - at_s, 0.0))
            made[j, j] = (score[cut[j], cut[j]] * spread * chosen).astype(BF16)
            if j + 1 < tiles:
                last = decay[:, (j + 1) * tile - 1 : (j + 1) * tile]
                fall = jnp.exp(last - at_s)
                for i in range(j + 1, tiles):
                    by = weight[(i ^ j).bit_length() + tile_bits][:, cut[i]] * jnp.exp(decay[:, cut[i]] - last)
                    made[j, i] = (score[cut[j], cut[i]] * fall * by).astype(BF16)
        v = vt[lines, :]
        parts = []
        empty = jnp.zeros((tile, tile), BF16)
        pair = min(2, tiles)
        for i in range(0, tiles, pair):
            cols = [
                jnp.concatenate([made.get((j, ii), empty) for j in range(i + pair)], axis=0)
                for ii in range(i, i + pair)
            ]
            parts.append(dot(v[:, : (i + pair) * tile], jnp.concatenate(cols, axis=1)))
        g = gt[lines, :].astype(F32)
        g = g / (1.0 + jnp.exp(-g))
        sg[lines, :] = g
        base[lines, :] = (jnp.concatenate(parts, axis=1) + skip_ref[h] * v.astype(F32)) * g
        return 0

    def receives(b):
        return bit_of(me, b)

    def sends(b):
        return jnp.logical_and(me + 2 < toks, bit_of(me + 2, b))

    def all_ones(first, last):
        value = me >= 0
        for b in range(first, last):
            value = jnp.logical_and(value, bit_of(me, b))
        return value

    def send_own(b, c):
        if b < tree:

            @pl.when(jnp.logical_and(jnp.logical_not(bit_of(me, b)), jnp.logical_and(sends(b), all_ones(1, b))))
            def _():
                state_copy(agg, b, c, lax.rem(me + 2, toks)).start()

    def comm(b, c):
        def each(fn):
            for h in range(c * per, (c + 1) * per):
                fn(h, slice(h * size, (h + 1) * size))

        if b == 0:
            state_copy(state, 0, c, partner).wait_recv()

            def join(h, s):
                mine, other = state[s], got[0, s]
                agg[s] = jnp.where(odd, other, mine) * fac_all[0, h : h + 1, :] + jnp.where(odd, mine, other)

            if tree > 1:
                each(join)
            send_own(1, c)
        else:

            @pl.when(receives(b))
            def _():
                state_copy(agg, b, c, lax.rem(me + 2, toks)).wait_recv()

                @pl.when(sends(b))
                def _():
                    state_copy(got.at[b], b, c, lax.rem(me + 2, toks)).start()

                if b + 1 < tree:

                    @pl.when(all_ones(1, b + 1))
                    def _():
                        def join(h, s):
                            agg[s] = got[b, s] * fac_all[b, h : h + 1, :] + agg[s]

                        each(join)
                        send_own(b + 1, c)

    def distant(b, c):
        @pl.when(receives(b))
        def _():
            s = slice(c * rows, (c + 1) * rows)
            lead = jnp.concatenate(
                [jnp.broadcast_to(fac_lead[b, h : h + 1, :], (size, depth)) for h in range(c * per, (c + 1) * per)], 0
            )
            x = got[b, s] * lead
            high = x.astype(BF16)
            low = (x - high.astype(F32)).astype(BF16)
            read = dot(jnp.concatenate([high, low], axis=1), qq[...])
            for h in range(per):
                hh = c * per + h
                by = w_ref[local_bits + 1 + b, hh : hh + 1, :] * jnp.exp(d_ref[hh : hh + 1, :])
                o = slice(hh * size, (hh + 1) * size)
                base[o] += read[h * size : (h + 1) * size] * by * sg[o]

    for k in range(chunks + tree - 1):
        if k < chunks:
            with jax.named_scope("near"):
                lax.fori_loop(k * per, (k + 1) * per, near, 0)
        if k == 0:
            for i in range(1, toks):
                tot_copy(me, lax.rem(me + i, toks)).wait_recv()
            for b in range(tree):
                start = lax.div(me, 1 << b) * (1 << b)
                lead = jnp.zeros(tot.shape[1:], F32)
                full = lead
                low = start if b else me + 1 - lax.rem(me, 2)
                for m in range(toks):
                    one = tot[m]
                    lead = lead + jnp.where(jnp.logical_and(m >= start, m < me), one, 0.0)
                    full = full + jnp.where(jnp.logical_and(m >= low, m < low + (1 << b)), one, 0.0)
                fac_lead[b] = jnp.exp(lead)
                fac_all[b] = jnp.exp(full)
        for b in range(tree):
            if 0 <= k - b < chunks:
                with jax.named_scope(f"exchange_{b}"):
                    comm(b, k - b)
        for b in range(tree):
            if 0 <= k - b < chunks:
                with jax.named_scope(f"distant_{b}"):
                    distant(b, k - b)

    with jax.named_scope("squares"):
        total = jnp.zeros((1, block), F32)
        for h in range(heads):
            g = base[h * size : (h + 1) * size]
            total = total + jnp.sum(g * g, axis=0, keepdims=True)

    ssq[my_head] = total

    def sq_copy(peer, slot):
        return pltpu.make_async_remote_copy(
            src_ref=ssq.at[slot], dst_ref=ssq.at[slot], send_sem=sq_send.at[peer], recv_sem=sq_recv.at[slot],
            device_id={"head": peer}, device_id_type=MESH,
        )

    for i in range(1, heads_ax):
        sq_copy(lax.rem(my_head + i, heads_ax), my_head).start()
    with jax.named_scope("turn"):
        turned[...] = base[...].T * gain_ref[...]

    with jax.named_scope("wait_squares"):
        for i in range(1, heads_ax):
            sq_copy(my_head, lax.rem(my_head + i, heads_ax)).wait_recv()

    with jax.named_scope("scale"):
        squares = ssq[0]
        for m in range(1, heads_ax):
            squares = squares + ssq[m]
        scaling = lax.rsqrt(squares / (width * heads_ax) + epsilon)
        for i in range(tiles):
            s = slice(i * tile, (i + 1) * tile)
            by = column(scaling[:, s], tile)
            for j in range(width // tile):
                c = slice(j * tile, (j + 1) * tile)
                out_ref[s, c] = (turned[s, c] * by).astype(BF16)

    for i in range(1, toks):
        tot_copy(lax.rem(me + i, toks), me).wait_send()
    for i in range(1, heads_ax):
        sq_copy(lax.rem(my_head + i, heads_ax), my_head).wait_send()
    for c in range(chunks):
        state_copy(state, 0, c, partner).wait_send()
    for b in range(1, tree):

        @pl.when(jnp.logical_and(sends(b), jnp.logical_or(bit_of(me, b), all_ones(1, b))))
        def _():
            for c in range(chunks):
                state_copy(agg, b, c, lax.rem(me + 2, toks)).wait_send()


def shards(toks, heads_ax, x, k, q, ld, w, skip, gate, gain):
    block, width = x.shape
    heads = ld.shape[1]
    depth = k.shape[1]
    tree = toks.bit_length() - 1
    tile = 128
    chunks = min(4, heads)
    vmem = pl.BlockSpec(memory_space=pltpu.VMEM)
    hbm = pl.BlockSpec(memory_space=pltpu.HBM)
    weight = w.transpose(2, 1, 0)
    return pl.pallas_call(
        functools.partial(kernel, (toks, heads_ax, tile, chunks)),
        out_shape=jax.ShapeDtypeStruct((block, width), BF16),
        in_specs=[hbm] * 5 + [pl.BlockSpec(memory_space=pltpu.SMEM), hbm, vmem],
        out_specs=vmem,
        scratch_shapes=[
            pltpu.VMEM(x.shape, BF16),
            pltpu.VMEM(k.shape, BF16),
            pltpu.VMEM(q.shape, BF16),
            pltpu.VMEM((heads, block), F32),
            pltpu.VMEM(weight.shape, F32),
            pltpu.VMEM(gate.shape, BF16),
            pltpu.SemaphoreType.DMA((6,)),
            pltpu.VMEM((heads, block), F32),
            pltpu.VMEM((toks, heads, depth), F32),
            pltpu.VMEM((tree, heads, depth), F32),
            pltpu.VMEM((tree, heads, depth), F32),
            pltpu.VMEM((width, depth), F32),
            pltpu.VMEM((width, depth), F32),
            pltpu.VMEM((tree, width, depth), F32),
            pltpu.VMEM((width, block), F32),
            pltpu.VMEM((width, block), F32),
            pltpu.VMEM((width, block), BF16),
            pltpu.VMEM((width, block), BF16),
            pltpu.VMEM((depth, block), F32),
            pltpu.VMEM((2 * depth, block), BF16),
            pltpu.VMEM((block, block), F32),
            pltpu.VMEM((block, width), F32),
            pltpu.VMEM((heads_ax, 1, block), F32),
            pltpu.SemaphoreType.DMA((toks,)),
            pltpu.SemaphoreType.DMA((toks,)),
            pltpu.SemaphoreType.DMA((tree, chunks)),
            pltpu.SemaphoreType.DMA((tree, chunks)),
            pltpu.SemaphoreType.DMA((heads_ax,)),
            pltpu.SemaphoreType.DMA((heads_ax,)),
        ],
        compiler_params=pltpu.CompilerParams(
            collective_id=0, has_side_effects=True, vmem_limit_bytes=60 * 2**20
        ),
    )(x, k, q, ld.T, weight, skip, gate, gain[None, :])


def solution(mesh):
    return jax.shard_map(
        functools.partial(shards, mesh.shape["tok"], mesh.shape["head"]),
        mesh=mesh,
        in_specs=(
            P("tok", "head"),
            P("tok", None),
            P("tok", None),
            P("tok", "head"),
            P("tok", "head", None),
            P("head"),
            P("tok", "head"),
            P("head"),
        ),
        out_specs=P("tok", "head"),
        check_vma=False,
    )
```
